256 devices in a mesh: dp: 32 (over z, y_hi, core), tensor: 8 (over y_lo, x).
Axes of the slice: x: 4, y: 4 (y_hi: 2, y_lo: 2; y = y_hi * 2 + y_lo), z: 8, core: 2. Of those that a mesh axis runs over, the one named last changes fastest.
Arguments:
- hidden: bfloat16 [16384, 24576], P('dp', 'tensor'), may hold values from -6 to 6
- down_grad: bfloat16 [24576, 6144], P('tensor', 'dp'), may hold values from -6 to 6
- old_inverse: float32 [8, 3072, 768], P('tensor', 'dp'), may hold values from -1 to 1
- owner: int32 [8, 4], P('tensor'), may hold values from 0 to 3, each once within a row
- damping: float32 [], replicated, may hold values from 0.05 to 0.5
Outputs:
- preconditioned: bfloat16 [24576, 6144], P('tensor', 'dp')
- new_inverse: float32 [8, 3072, 768], P('tensor', 'dp')
The draws below stay inside these ranges and needn't reach their ends.
All inputs are finite; a program needn't handle non-finite values.
Results may differ from the reference program's by a relative error of at most 0.02.
Values may be sent and summed in bfloat16 or wider, within the bound.
A program may use at most 64 MiB of HBM per device.

```python
import math
import jax
import jax.numpy as jnp
from jax import lax

D = 6144
FF = 24576
B = 768
ITERS = 3
TOKENS = 16384
NBLK = 4
N_TENSOR = 8


def draw_old_inverse(key, part):
    key = jax.random.fold_in(key, 11)
    noise = jax.random.normal(key, (N_TENSOR, FF // N_TENSOR, B), jnp.float32)
    row_pos = jnp.arange(FF // N_TENSOR) % B
    diag_mask = (row_pos[:, None] == jnp.arange(B)[None, :]).astype(jnp.float32)
    return 0.4 * diag_mask[None] + 0.1 / math.sqrt(B) * noise


def draw_hidden(key, part):
    key = jax.random.fold_in(key, 23)
    key_base = jax.random.fold_in(key, 0)
    values = jnp.clip(jax.random.normal(key_base, (TOKENS, FF), jnp.float32), -6.0, 6.0)
    return values.astype(jnp.bfloat16)


def block_scale(own_key, extent, shards, least, high):
    level, own = 1.0, jax.random.fold_in(own_key, 6)
    for position, parts in shards:
        draws = jnp.exp(jax.random.uniform(jax.random.fold_in(own, position), (parts,), jnp.float32, least / len(shards), high / len(shards)))
        level = level * jnp.repeat(draws, extent[position] // parts).reshape([-1 if axis == position else 1 for axis in range(len(extent))])
    return level


def bell_draw(stream_key, dims, scale, bound, cuts=(), kind=jnp.bfloat16):
    values = scale * jax.random.normal(stream_key, dims, jnp.float32)
    if cuts:
        values = values * block_scale(stream_key, dims, cuts, -0.22, 0.18)
    return jnp.clip(values, -bound, bound).astype(kind)


def setup_inputs(seed: int = 0) -> dict:
    seeds = jax.random.split(jax.random.key(seed), 6)
    return {
        "hidden": draw_hidden(jax.random.fold_in(seeds[5], 71), 0),
        "down_grad": bell_draw(seeds[1], (FF, D), 1.0, 6.0, ((0, 8), (1, 32))),
        "old_inverse": draw_old_inverse(jax.random.fold_in(seeds[5], 71), 0),
        "owner": jax.vmap(lambda own: jax.random.permutation(own, NBLK))(jax.random.split(seeds[3], N_TENSOR)).reshape((N_TENSOR, NBLK)).astype(jnp.int32),
        "damping": jnp.clip(jnp.exp(jax.random.uniform(seeds[4], (), jnp.float32, math.log(0.05), math.log(0.5))), 0.05, 0.5),
    }


def reference(hidden, down_grad, old_inverse, owner, damping):
    tokens = hidden.shape[0]
    local_cols = FF // N_TENSOR
    blk_count = local_cols // B
    identity = jnp.eye(B, dtype=jnp.float32)
    inverses = []
    results = []
    for tensor_idx in range(N_TENSOR):
        columns = hidden[:, tensor_idx * local_cols:(tensor_idx + 1) * local_cols].astype(jnp.float32)
        columns = columns.reshape(tokens, blk_count, B)
        statistic = jnp.einsum("tkb,tkc->kbc", columns, columns, precision=lax.Precision.HIGHEST)
        statistic = statistic / tokens + damping * identity
        slot_ids = owner[tensor_idx]
        warm_start = old_inverse[tensor_idx].reshape(blk_count, B, B)[slot_ids]
        current = warm_start
        for newton_step in range(ITERS):
            product = jnp.matmul(statistic, current, precision=lax.Precision.HIGHEST)
            current = 2.0 * current - jnp.matmul(current, product, precision=lax.Precision.HIGHEST)
        stored = jnp.zeros((blk_count, B, B), jnp.float32).at[slot_ids].set(current)
        inverses.append(stored.reshape(local_cols, B))
        lowered = current.astype(jnp.bfloat16).astype(jnp.float32)
        grad_rows = down_grad[tensor_idx * local_cols:(tensor_idx + 1) * local_cols].astype(jnp.float32)
        grad_rows = grad_rows.reshape(blk_count, B, D)
        precond = jnp.einsum("kij,kjd->kid", lowered, grad_rows, precision=lax.Precision.HIGHEST)
        results.append(precond.astype(jnp.bfloat16).reshape(local_cols, D))
    return jnp.concatenate(results, 0), jnp.stack(inverses, 0)
```

```python
import jax
import jax.numpy as jnp
from jax import lax
from jax.experimental import pallas as pl
from jax.experimental.pallas import tpu as pltpu
from jax.sharding import PartitionSpec as P

MESH = pl.DeviceIdType.MESH
B = 768
T = 128
NT = B // T
PACK = NT * (NT + 1) // 2 * T
Z = 8
SHARD = PACK // Z
CUT = 176
WROWS = 96
WCUT = 48
COLS = 192
TOKENS = 16384
N_MSG = 80
BF = jnp.bfloat16
F32 = jnp.float32


def dot(a, b):
    return jnp.dot(a, b, preferred_element_type=F32)


def tile_rows(bi, bj):
    start = (bi * (bi + 1) // 2 + bj) * T
    return slice(start, start + T)


def kernel(
    owner, damping, hid, grad, old, out, inv,
    h, pf, ps, pr, rs_s, rs_r, col, ys, yr, spk, w, wf, sf, x0, rb, r2, gown, gsib, gc, av, w1, wb, yv, yown, ysib,
    chain_f, chain_b, inv_s, inv_r, inv_o, loc, send, recv,
):
    me = lax.axis_index("dp")
    tens = lax.axis_index("tensor")
    z, yh, c = me // 4, me // 2 % 2, me % 2

    def ring(shift):
        return lax.rem(z + shift % Z, Z)

    up = (ring(1) * 4 + yh * 2 + c, tens)
    down = (ring(-1) * 4 + yh * 2 + c, tens)
    across = (z * 4 + (1 - yh) * 2 + c, tens)
    sib = (z * 4 + yh * 2 + 1 - c, tens)
    dirs = (down, up)
    count = [0]
    sent = []

    class Message:
        def __init__(self, src, dst, device, land=None):
            n = count[0]
            count[0] += 1
            self.copy = pltpu.make_async_remote_copy(
                src_ref=src, dst_ref=dst, send_sem=send.at[n], recv_sem=recv.at[n], device_id=device, device_id_type=MESH
            )
            land = dst if land is None else land
            self.arrival = pltpu.make_async_remote_copy(
                src_ref=land, dst_ref=land, send_sem=send.at[n], recv_sem=recv.at[n], device_id=device, device_id_type=MESH
            )
            self.copy.start()
            sent.append(self)

        def wait(self):
            self.arrival.wait_recv()

    hid_copies = []
    for q in range(4):
        block = 2 * (1 - c) + q if q < 2 else 2 * c + q - 2
        cp = pltpu.make_async_copy(hid.at[:, pl.ds(pl.multiple_of(block * B, B), B)], h.at[q], loc.at[q])
        cp.start()
        hid_copies.append(cp)
    old_copy = pltpu.make_async_copy(old.at[0], wf, loc.at[4])
    old_copy.start()
    own_rows = pl.ds(pl.multiple_of(c * 2 * B, 2 * B), 2 * B)
    sib_rows = pl.ds(pl.multiple_of((1 - c) * 2 * B, 2 * B), 2 * B)
    gown_copy = pltpu.make_async_copy(grad.at[own_rows, :], gown, loc.at[5])
    gown_copy.start()

    barrier = pltpu.get_barrier_semaphore()
    for device in (up, down, across, sib):
        pl.semaphore_signal(barrier, inc=1, device_id=device, device_id_type=MESH)

    def gram(q):
        hid_copies[q].wait()
        for i in range(B // 256):
            left = h[q, :, 256 * i : 256 * i + 256].T
            block = dot(left, h[q, :, 0 : 256 * i + 256])
            for a in range(2):
                bi = 2 * i + a
                for bj in range(bi + 1):
                    tile = block[T * a : T * a + T, T * bj : T * bj + T]
                    if q < 2:
                        ps[q, tile_rows(bi, bj), :] = tile.astype(BF)
                    else:
                        pf[q - 2, tile_rows(bi, bj), :] = tile

    gram(0)
    pl.semaphore_wait(barrier, 4)
    m_stat = [Message(ps.at[0], pr.at[0], sib)]
    old_copy.wait()
    w[z, yh, c] = wf[...].astype(BF)

    def w_cross(origin):
        return Message(w.at[origin, yh, c], w.at[origin, yh, c], across, land=w.at[origin, 1 - yh, c])

    def w_step(t):
        messages = []
        for d, sign in ((0, -1), (1, 1)):
            origin, arriving = ring(-sign * (t - 1)), ring(-sign * t)
            rows = slice(0, WROWS) if t < 4 else (slice(0, WCUT), slice(WCUT, WROWS))[d]
            messages.append(Message(w.at[origin, yh, c, rows], w.at[origin, yh, c, rows], dirs[d], land=w.at[arriving, yh, c, rows]))
        return messages

    m_w = w_step(1)
    m_wy = [w_cross(z)]
    m_grad = Message(grad.at[sib_rows, :], gsib, sib)

    gram(1)
    m_stat.append(Message(ps.at[1], pr.at[1], sib))
    gram(2)

    def shard(dest):
        return pl.ds(pl.multiple_of(dest * SHARD, SHARD), SHARD)

    def own(j, dest):
        rows = shard(dest)
        return pf[j, rows, :] + pr[j, rows, :].astype(F32)

    def rs_step(j, t, before):
        messages = []
        if t == 1:
            m_stat[j].wait()
            part = own(j, ring(4)).astype(BF)
            for d, rows in ((0, slice(0, CUT)), (1, slice(CUT, SHARD))):
                rs_s[j, d, 0, rows, :] = part[rows]
                messages.append(Message(rs_s.at[j, d, 0, rows], rs_r.at[j, d, 0, rows], dirs[d]))
            return messages
        for d, sign in ((0, -1), (1, 1)):
            part = own(j, ring(sign * (5 - t)))
            before[d].wait()
            if t == 2:
                rows = (slice(0, CUT), slice(CUT, SHARD))[d]
                other = (slice(CUT, SHARD), slice(0, CUT))[d]
                rs_s[j, d, t - 1, other, :] = part[other].astype(BF)
                rs_s[j, d, t - 1, rows, :] = (part[rows] + rs_r[j, d, 0, rows, :].astype(F32)).astype(BF)
            else:
                rs_s[j, d, t - 1] = (part + rs_r[j, d, t - 2].astype(F32)).astype(BF)
            messages.append(Message(rs_s.at[j, d, t - 1], rs_r.at[j, d, t - 1], dirs[d]))
        return messages

    def rs_end(j, before):
        part = own(j, z)
        for d in range(2):
            before[d].wait()
            part = part + rs_r[j, d, 3].astype(F32)
        col[j] = part
        ys[j] = part.astype(BF)
        return Message(ys.at[j], yr.at[j], across)

    def ag_step(j, t, before):
        messages = []
        for d, sign in ((0, -1), (1, 1)):
            if t > 1:
                before[d].wait()
            origin, arriving = ring(-sign * (t - 1)), ring(-sign * t)
            lo, size = (0, SHARD) if t < 4 else ((0, CUT), (CUT, SHARD - CUT))[d]
            rows = pl.ds(pl.multiple_of(origin * SHARD + lo, 16), size)
            land = pl.ds(pl.multiple_of(arriving * SHARD + lo, 16), size)
            messages.append(Message(spk.at[j, rows], spk.at[j, rows], dirs[d], land=spk.at[j, land]))
        return messages

    rs = [None, None]
    rs[0] = rs_step(0, 1, None)
    gram(3)
    rs[1] = rs_step(1, 1, None)

    def w_forward(t):
        nonlocal m_w
        for m in m_w:
            m.wait()
        m_w = w_step(t)
        m_wy.append(w_cross(ring(1 - t)))
        m_wy.append(w_cross(ring(t - 1)))

    w_forward(2)
    rs[0] = rs_step(0, 2, rs[0])
    rs[1] = rs_step(1, 2, rs[1])
    w_forward(3)
    rs[0] = rs_step(0, 3, rs[0])
    rs[1] = rs_step(1, 3, rs[1])
    w_forward(4)
    rs[0] = rs_step(0, 4, rs[0])
    rs[1] = rs_step(1, 4, rs[1])
    for m in m_w:
        m.wait()
    m_wy.append(w_cross(ring(4)))
    m_wd = [Message(w.at[:, yh, c], w.at[:, yh, c], sib, land=w.at[:, yh, 1 - c])]

    m_y = [rs_end(0, rs[0]), rs_end(1, rs[1])]

    gown_copy.wait()
    m_grad.wait()
    for j in range(2):
        rows = slice(j * B, j * B + B)
        gc[j] = jnp.concatenate([gown[rows, :], gsib[rows, :]], axis=1)

    ag = [None, None]
    for j in range(2):
        m_y[j].wait()
        spk[j, shard(z), :] = (col[j] + yr[j].astype(F32)).astype(BF)
        ag[j] = ag_step(j, 1, None)
    for t in (2, 3):
        for j in range(2):
            ag[j] = ag_step(j, t, ag[j])
    ag[0] = ag_step(0, 4, ag[0])
    ag[1] = ag_step(1, 4, ag[1])

    for m in m_wy:
        m.wait()
    m_wd.append(Message(w.at[:, 1 - yh, c], w.at[:, 1 - yh, c], sib, land=w.at[:, 1 - yh, 1 - c]))
    for m in m_wd:
        m.wait()
    for j in range(2):
        slot = owner[0, 2 * c + j]
        x0[j] = w[pl.ds(2 * slot, 2)].reshape(B, B)

    damp = damping[0, 0]

    def residual(j):
        for m in ag[j]:
            m.wait()
        for bi in range(NT):
            for bj in range(bi + 1):
                tile = spk[j, tile_rows(bi, bj), :]
                sf[T * bi : T * bi + T, T * bj : T * bj + T] = tile
                if bj < bi:
                    sf[T * bj : T * bj + T, T * bi : T * bi + T] = tile.T
        product = dot(sf[...], x0[j])
        diagonal = lax.broadcasted_iota(jnp.int32, (B, B), 0) == lax.broadcasted_iota(jnp.int32, (B, B), 1)
        left = jnp.where(diagonal, 1.0, 0.0) - product * (1.0 / TOKENS) - damp * x0[j].astype(F32)
        rb[j] = left.astype(BF)
        r2[j] = dot(rb[j], rb[j]).astype(BF)

    def apply(j):
        av[...] = dot(r2[j], gc[j]).astype(BF)
        first = gc[j].astype(F32) + dot(r2[j], av[...])
        w1[...] = first
        wb[...] = first.astype(BF)
        second = w1[...] + dot(r2[j], wb[...])
        w1[...] = second
        av[...] = second.astype(BF)
        third = w1[...] + dot(rb[j], av[...])
        wb[...] = third.astype(BF)
        yv[...] = dot(x0[j], wb[...]).astype(BF)
        yown[j] = yv[:, :COLS]
        ysib[j] = yv[:, COLS:]
        rows = pl.ds(pl.multiple_of((2 * c + j) * B, B), B)
        store = pltpu.make_async_copy(yown.at[j], out.at[rows, :], loc.at[6 + j])
        store.start()
        land = pl.ds(pl.multiple_of((2 * (1 - c) + j) * B, B), B)
        return store, Message(ysib.at[j], out.at[rows, :], sib, land=out.at[land, :])

    residual(0)
    done = [apply(0)]
    residual(1)

    slot = z // 2
    block = jnp.int32(0)
    for k in range(4):
        block = jnp.where(owner[0, k] == slot, k, block)
    here = block // 2 == c
    jj = block % 2
    start = w[z].reshape(2, 2 * WROWS, B)
    chain_f[...] = start.reshape(4 * WROWS, B).astype(F32)
    chain_b[...] = start.reshape(4 * WROWS, B)
    mine = pl.ds(pl.multiple_of(yh * 2 * WROWS, 2 * WROWS), 2 * WROWS)
    rows_b = chain_b[mine, :]
    u = chain_f[mine, :] + dot(rows_b, rb[jj])
    u = u + dot(u.astype(BF), r2[jj])
    v = dot(u.astype(BF), r2[jj])
    u = u + dot(v.astype(BF), r2[jj])
    inv_s[...] = u
    m_inv = Message(
        inv_s.at[pl.ds(pl.multiple_of((1 - c) * WROWS, WROWS), WROWS)], inv_r, sib
    )
    done.append(apply(1))
    m_inv.wait()
    own_part = inv_s[pl.ds(pl.multiple_of(c * WROWS, WROWS), WROWS), :]
    inv_o[...] = jnp.where(here, own_part, inv_r[...])
    inv_store = pltpu.make_async_copy(inv_o, inv.at[0], loc.at[8])
    inv_store.start()
    for store, message in done:
        store.wait()
        message.wait()
    inv_store.wait()
    for message in sent:
        message.copy.wait_send()


def body(hidden, down_grad, old_inverse, owner, damping):
    V = pltpu.VMEM
    any_space = pl.BlockSpec(memory_space=pl.ANY)
    smem = pl.BlockSpec(memory_space=pltpu.SMEM)
    return pl.pallas_call(
        kernel,
        out_shape=(
            jax.ShapeDtypeStruct(down_grad.shape, BF),
            jax.ShapeDtypeStruct(old_inverse.shape, F32),
        ),
        in_specs=[smem, smem, any_space, any_space, any_space],
        out_specs=(any_space, any_space),
        scratch_shapes=[
            V((4, hidden.shape[0], B), BF),
            V((2, PACK, T), F32),
            V((2, PACK, T), BF),
            V((2, PACK, T), BF),
            V((2, 2, 4, SHARD, T), BF),
            V((2, 2, 4, SHARD, T), BF),
            V((2, SHARD, T), F32),
            V((2, SHARD, T), BF),
            V((2, SHARD, T), BF),
            V((2, PACK, T), BF),
            V((Z, 2, 2, WROWS, B), BF),
            V((WROWS, B), F32),
            V((B, B), BF),
            V((2, B, B), BF),
            V((2, B, B), BF),
            V((2, B, B), BF),
            V((2 * B, COLS), BF),
            V((2 * B, COLS), BF),
            V((2, B, 2 * COLS), BF),
            V((B, 2 * COLS), BF),
            V((B, 2 * COLS), F32),
            V((B, 2 * COLS), BF),
            V((B, 2 * COLS), BF),
            V((2, B, COLS), BF),
            V((2, B, COLS), BF),
            V((4 * WROWS, B), F32),
            V((4 * WROWS, B), BF),
            V((2 * WROWS, B), F32),
            V((WROWS, B), F32),
            V((WROWS, B), F32),
            pltpu.SemaphoreType.DMA((16,)),
            pltpu.SemaphoreType.DMA((N_MSG,)),
            pltpu.SemaphoreType.DMA((N_MSG,)),
        ],
        compiler_params=pltpu.CompilerParams(collective_id=0, has_side_effects=True, vmem_limit_bytes=60 << 20),
    )(owner, damping.reshape(1, 1), hidden, down_grad, old_inverse)


def solution(mesh):
    in_specs = (
        P("dp", "tensor"),
        P("tensor", "dp"),
        P("tensor", "dp", None),
        P("tensor", None),
        P(),
    )
    out_specs = (P("tensor", "dp"), P("tensor", "dp", None))
    return jax.shard_map(body, mesh=mesh, in_specs=in_specs, out_specs=out_specs, check_vma=False)
```

```python
import jax
import jax.numpy as jnp
from jax import lax
from jax.experimental import pallas as pl
from jax.experimental.pallas import tpu as pltpu
from jax.sharding import PartitionSpec as P

MESH = pl.DeviceIdType.MESH
B = 768
T = 128
NT = B // T
PACK = (NT * (NT - 1) // 2 + NT // 2 + 1) * T
Z = 8
SHARD = PACK // Z
WROWS = 96
WCUT = 48
COLS = 192
TOKENS = 16384
N_MSG = 140
WARM = ((0, 48, 32), (48, 48, 16))
BF = jnp.bfloat16
F32 = jnp.float32


def dot(a, b):
    return jnp.dot(a, b, preferred_element_type=F32)


def tile_rows(bi, bj):
    start = (bi * (bi - 1) // 2 + bj) * T
    return slice(start, start + T)


def fold_rows(i):
    start = (NT * (NT - 1) // 2 + i) * T
    return slice(start, start + T)


LAST = fold_rows(NT // 2)


PIECES = (((0, 160, 80), (160, 144, 64)), ((0, 160, 80), (160, 144, 64)))
PLAN = (
    "G0", "bar", "P0", "W", "V", "grad", "G1", "P1", "G2", "S0", "ab", "G3", "S1", "W", "ab", "cd", "V",
    "ab", "cd", "W", "ab", "cd", "V", "ab", "cd", "W", "ab", "cd", "V", "ab", "cd", "W", "V", "ab", "cd",
    "gw", "W", "V", "ab", "cd", "x", "AA", "cd", "AAAAA", "cd", "BBB", "N", "BBBB", "N", "N",
)


def nt_dot(a, b):
    return lax.dot_general(a, b, (((1,), (1,)), ((), ())), preferred_element_type=F32)


def kernel(
    owner, damping, hid, grad, old, out, inv,
    h, pf, ps, pr, rs_s, rs_r, col, ys, yr, spk, w, wf, sf, x0, q1, q2, gt, av, w1, wb, yt,
    g0, inv_s, inv_r, inv_o, loc, send, recv,
):
    me = lax.axis_index("dp")
    tens = lax.axis_index("tensor")
    z, yh, c = me // 4, me // 2 % 2, me % 2

    def ring(shift):
        return lax.rem(z + shift % Z, Z)

    up = (ring(1) * 4 + yh * 2 + c, tens)
    down = (ring(-1) * 4 + yh * 2 + c, tens)
    across = (z * 4 + (1 - yh) * 2 + c, tens)
    sib = (z * 4 + yh * 2 + 1 - c, tens)
    dirs = (down, up)
    sent = []

    class Message:
        def __init__(self, src, dst, device, land=None):
            n = len(sent)
            self.copy = pltpu.make_async_remote_copy(
                src_ref=src, dst_ref=dst, send_sem=send.at[n], recv_sem=recv.at[n], device_id=device, device_id_type=MESH
            )
            land = dst if land is None else land
            self.arrival = pltpu.make_async_remote_copy(
                src_ref=land, dst_ref=land, send_sem=send.at[n], recv_sem=recv.at[n], device_id=device, device_id_type=MESH
            )
            self.arrived = False
            self.copy.start()
            sent.append(self)

        def wait(self):
            self.arrived = True
            self.arrival.wait_recv()

    class Load:
        def __init__(self, src, dst, n):
            self.copy = pltpu.make_async_copy(src, dst, loc.at[n])
            self.copy.start()
            self.waited = False
            loads.append(self)

        def wait(self):
            self.waited = True
            self.copy.wait()

    loads = []
    hid_copies = []
    for q in range(4):
        block = 2 * (1 - c) + q if q < 2 else 2 * c + q - 2
        hid_copies.append(Load(hid.at[:, pl.ds(pl.multiple_of(block * B, B), B)], h.at[q], q))
    old_copy = Load(old.at[0], wf, 4)

    def columns(core, j):
        return pl.ds(pl.multiple_of((2 * core + j) * B, B), B)

    grad_copies = [Load(grad.at[:, columns(c, j)], gt.at[j, 0:COLS], 5 + j) for j in range(2)]

    barrier = pltpu.get_barrier_semaphore()
    for device in (up, down, across, sib):
        pl.semaphore_signal(barrier, inc=1, device_id=device, device_id_type=MESH)

    row = lax.broadcasted_iota(jnp.int32, (T, T), 0)
    column = lax.broadcasted_iota(jnp.int32, (T, T), 1)

    def gram(q):
        hid_copies[q].wait()

        def put(rows, tile):
            if q < 2:
                ps[q, rows, :] = tile.astype(BF)
            else:
                pf[q - 2, rows, :] = tile

        last = jnp.zeros((T, T), F32)
        for i in range(B // 256):
            left = h[q, :, 256 * i : 256 * i + 256].T
            block = dot(left, h[q, :, 0 : 256 * i + 256])
            for a in range(2):
                bi = 2 * i + a
                for bj in range(bi):
                    put(tile_rows(bi, bj), block[T * a : T * a + T, T * bj : T * bj + T])
            lower = block[0:T, 256 * i : 256 * i + T]
            upper = block[T:, 256 * i + T :]
            put(fold_rows(i), jnp.where(row >= column, lower, upper))
            last = jnp.where(row == i, jnp.sum(jnp.where(row == column, upper, 0.0), axis=0, keepdims=True), last)
        put(LAST, last)

    def warm(lo, size, cut):
        every = slice(lo, lo + size)

        def cross(origin):
            return Message(w.at[origin, yh, c, every], w.at[origin, yh, c, every], across, land=w.at[origin, 1 - yh, c, every])

        def step(t):
            messages = []
            for d, sign in ((0, -1), (1, 1)):
                origin, arriving = ring(-sign * (t - 1)), ring(-sign * t)
                rows = every if t < 4 else (slice(lo, lo + cut), slice(lo + cut, lo + size))[d]
                messages.append(
                    Message(w.at[origin, yh, c, rows], w.at[origin, yh, c, rows], dirs[d], land=w.at[arriving, yh, c, rows])
                )
            return messages

        ringed = step(1)
        crossed = [cross(z)]
        yield
        for t in (2, 3, 4):
            for m in ringed:
                m.wait()
            ringed = step(t)
            crossed += [cross(ring(1 - t)), cross(ring(t - 1))]
            yield
        for m in ringed:
            m.wait()
        crossed.append(cross(ring(4)))
        swapped = [Message(w.at[:, yh, c, every], w.at[:, yh, c, every], sib, land=w.at[:, yh, 1 - c, every])]
        yield
        for m in crossed:
            m.wait()
        swapped.append(
            Message(w.at[:, 1 - yh, c, every], w.at[:, 1 - yh, c, every], sib, land=w.at[:, 1 - yh, 1 - c, every])
        )
        yield
        for m in swapped:
            m.wait()
        yield

    def stream(j, lo, size, cut):
        def rows_of(dest, first=0, count=size):
            return pl.ds(pl.multiple_of(dest * SHARD + lo + first, 16), count)

        def own(dest):
            rows = rows_of(dest)
            return pf[j, rows, :] + pr[j, rows, :].astype(F32)

        here = slice(lo, lo + size)
        halves = (slice(0, cut), slice(cut, size))
        placed = (slice(lo, lo + cut), slice(lo + cut, lo + size))
        part = own(ring(4)).astype(BF)
        before = []
        for d in range(2):
            rs_s[j, d, 0, placed[d], :] = part[halves[d]]
            before.append(Message(rs_s.at[j, d, 0, placed[d]], rs_r.at[j, d, 0, placed[d]], dirs[d]))
        yield
        for t in (2, 3, 4):
            after = []
            for d, sign in ((0, -1), (1, 1)):
                part = own(ring(sign * (5 - t)))
                before[d].wait()
                if t == 2:
                    rs_s[j, d, 1, placed[1 - d], :] = part[halves[1 - d]].astype(BF)
                    rs_s[j, d, 1, placed[d], :] = (part[halves[d]] + rs_r[j, d, 0, placed[d], :].astype(F32)).astype(BF)
                else:
                    rs_s[j, d, t - 1, here, :] = (part + rs_r[j, d, t - 2, here, :].astype(F32)).astype(BF)
                after.append(Message(rs_s.at[j, d, t - 1, here], rs_r.at[j, d, t - 1, here], dirs[d]))
            before = after
            yield
        part = own(z)
        for d in range(2):
            before[d].wait()
            part = part + rs_r[j, d, 3, here, :].astype(F32)
        col[j, here, :] = part
        ys[j, here, :] = part.astype(BF)
        crossed = Message(ys.at[j, here], yr.at[j, here], across)
        yield
        crossed.wait()
        spk[j, rows_of(z), :] = (col[j, here, :] + yr[j, here, :].astype(F32)).astype(BF)
        for t in (1, 2, 3, 4):
            after = []
            for d, sign in ((0, -1), (1, 1)):
                if t > 1:
                    before[d].wait()
                origin, arriving = ring(-sign * (t - 1)), ring(-sign * t)
                first, count = (0, size) if t < 4 else ((0, cut), (cut, size - cut))[d]
                src, land = rows_of(origin, first, count), rows_of(arriving, first, count)
                after.append(Message(spk.at[j, src], spk.at[j, src], dirs[d], land=spk.at[j, land]))
            before = after
            yield
        for m in before:
            m.wait()
        yield

    damp = damping[0, 0]
    tail = {}
    first_row = (z % 2) * 4 * WROWS + yh * 2 * WROWS

    def prepare():
        for name in "WV":
            for _ in runs.get(name, ()):
                pass
        for j in range(2):
            slot = owner[0, 2 * c + j]
            x0[j] = w[pl.ds(2 * slot, 2)].reshape(B, B)
        for j in range(2):
            g0[j] = nt_dot(gt[j], x0[j])

    def refine(j):
        for name in piece_names[j]:
            for _ in runs.get(name, ()):
                pass
        for bi in range(NT):
            for bj in range(bi):
                tile = spk[j, tile_rows(bi, bj), :]
                sf[T * bi : T * bi + T, T * bj : T * bj + T] = tile
                sf[T * bj : T * bj + T, T * bi : T * bi + T] = tile.T
        last = spk[j, LAST, :].astype(F32)
        for i in range(NT // 2):
            tile = spk[j, fold_rows(i), :].astype(F32)
            turned = tile.T
            at = slice(256 * i, 256 * i + T)
            sf[at, at] = jnp.where(row >= column, tile, turned).astype(BF)
            at = slice(256 * i + T, 256 * i + 256)
            rest = jnp.where(row > column, turned, last[i : i + 1, :])
            sf[at, at] = jnp.where(row < column, tile, rest).astype(BF)
        yield
        product = dot(x0[j], sf[...])
        diagonal = lax.broadcasted_iota(jnp.int32, (B, B), 0) == lax.broadcasted_iota(jnp.int32, (B, B), 1)
        left = jnp.where(diagonal, 1.0, 0.0) - product * (1.0 / TOKENS) - damp * x0[j].astype(F32)
        q1[j] = left.astype(BF)
        yield
        q2[j] = dot(q1[j], q1[j]).astype(BF)
        yield
        first = g0[j] + nt_dot(g0[j].astype(BF), q1[j])
        w1[...] = first
        wb[...] = first.astype(BF)
        yield
        second = w1[...] + nt_dot(wb[...], q2[j])
        w1[...] = second
        av[...] = second.astype(BF)
        yield
        wb[...] = nt_dot(av[...], q2[j]).astype(BF)
        yield
        yt[j] = (w1[...] + nt_dot(wb[...], q2[j])).astype(BF)
        store = pltpu.make_async_copy(yt.at[j, 0:COLS], out.at[:, columns(c, j)], loc.at[7 + j])
        store.start()
        tail[j] = store, Message(
            yt.at[j, COLS : 2 * COLS], out.at[:, columns(c, j)], sib, land=out.at[:, columns(1 - c, j)]
        )
        yield

    def inverse_rows():
        slot = z // 2
        block = jnp.int32(0)
        for k in range(4):
            block = jnp.where(owner[0, k] == slot, k, block)
        jj = block % 2
        shape = (2 * WROWS, B)
        unit = lax.broadcasted_iota(jnp.int32, shape, 0) + first_row == lax.broadcasted_iota(jnp.int32, shape, 1)
        mine = q1[jj, pl.ds(pl.multiple_of(first_row, 2 * WROWS), 2 * WROWS), :]
        u = jnp.where(unit, 1.0, 0.0) + mine.astype(F32)
        u = u + dot(u.astype(BF), q2[jj])
        v = dot(u.astype(BF), q2[jj])
        u = u + dot(v.astype(BF), q2[jj])
        inv_s[...] = dot(u.astype(BF), x0[jj])
        message = Message(inv_s.at[pl.ds(pl.multiple_of((1 - c) * WROWS, WROWS), WROWS)], inv_r, sib)
        yield
        message.wait()
        own_part = inv_s[pl.ds(pl.multiple_of(c * WROWS, WROWS), WROWS), :]
        inv_o[...] = jnp.where(block // 2 == c, own_part, inv_r[...])
        store = pltpu.make_async_copy(inv_o, inv.at[0], loc.at[9])
        store.start()
        yield
        store.wait()
        yield

    runs = {"N": inverse_rows(), "A": refine(0), "B": refine(1)}
    piece_names = ("ab", "cd")
    for name, piece in zip("WV", WARM):
        runs[name] = warm(*piece)
    for j in range(2):
        for name, piece in zip(piece_names[j], PIECES[j]):
            runs[name] = stream(j, *piece)
    stat = []
    for step in PLAN:
        if step[0] == "G":
            gram(int(step[1]))
        elif step[0] == "P":
            q = int(step[1])
            stat.append(Message(ps.at[q], pr.at[q], sib))
        elif step == "bar":
            pl.semaphore_wait(barrier, 4)
            old_copy.wait()
            w[z, yh, c] = wf[...].astype(BF)
        elif step == "x":
            prepare()
        elif step[0] == "S":
            stat[int(step[1])].wait()
        elif step == "grad":
            grads = [
                Message(grad.at[:, columns(1 - c, j)], gt.at[j, COLS : 2 * COLS], sib) for j in range(2)
            ]
        elif step == "gw":
            for j in range(2):
                grad_copies[j].wait()
                grads[j].wait()
        else:
            for name in step:
                next(runs.get(name, iter(())), None)
    for j in tail:
        tail[j][0].wait()
    for load in loads:
        if not load.waited:
            load.wait()
    for message in sent:
        if not message.arrived:
            message.wait()
    for message in sent:
        message.copy.wait_send()


def body(hidden, down_grad, old_inverse, owner, damping):
    V = pltpu.VMEM
    any_space = pl.BlockSpec(memory_space=pl.ANY)
    smem = pl.BlockSpec(memory_space=pltpu.SMEM)
    result, inverse = pl.pallas_call(
        kernel,
        out_shape=(
            jax.ShapeDtypeStruct(down_grad.shape[::-1], BF),
            jax.ShapeDtypeStruct(old_inverse.shape, F32),
        ),
        in_specs=[smem, smem, any_space, any_space, any_space],
        out_specs=(any_space, any_space),
        scratch_shapes=[
            V((4, hidden.shape[0], B), BF),
            V((2, PACK, T), F32),
            V((2, PACK, T), BF),
            V((2, PACK, T), BF),
            V((2, 2, 4, SHARD, T), BF),
            V((2, 2, 4, SHARD, T), BF),
            V((2, SHARD, T), F32),
            V((2, SHARD, T), BF),
            V((2, SHARD, T), BF),
            V((2, PACK, T), BF),
            V((Z, 2, 2, WROWS, B), BF),
            V((WROWS, B), F32),
            V((B, B), BF),
            V((2, B, B), BF),
            V((2, B, B), BF),
            V((2, B, B), BF),
            V((2, 2 * COLS, B), BF),
            V((2 * COLS, B), BF),
            V((2 * COLS, B), F32),
            V((2 * COLS, B), BF),
            V((2, 2 * COLS, B), BF),
            V((2, 2 * COLS, B), F32),
            V((2 * WROWS, B), F32),
            V((WROWS, B), F32),
            V((WROWS, B), F32),
            pltpu.SemaphoreType.DMA((16,)),
            pltpu.SemaphoreType.DMA((N_MSG,)),
            pltpu.SemaphoreType.DMA((N_MSG,)),
        ],
        compiler_params=pltpu.CompilerParams(collective_id=0, has_side_effects=True, vmem_limit_bytes=60 << 20),
    )(owner, damping.reshape(1, 1), hidden, down_grad.T, old_inverse)
    return result.T, inverse


def solution(mesh):
    in_specs = (
        P("dp", "tensor"),
        P("tensor", "dp"),
        P("tensor", "dp", None),
        P("tensor", None),
        P(),
    )
    out_specs = (P("tensor", "dp"), P("tensor", "dp", None))
    return jax.shard_map(body, mesh=mesh, in_specs=in_specs, out_specs=out_specs, check_vma=False)
```

```python
import jax
import jax.numpy as jnp
from jax import lax
from jax.experimental import pallas as pl
from jax.experimental.pallas import tpu as pltpu
from jax.sharding import PartitionSpec as P

MESH = pl.DeviceIdType.MESH
B = 768
T = 128
NT = B // T
PACK = (NT * (NT - 1) // 2 + NT // 2 + 1) * T
Z = 8
SHARD = PACK // Z
WROWS = 96
WCUT = 48
COLS = 192
TOKENS = 16384
N_MSG = 140
KEEP = 30
WARM = ((0, 48, 32), (48, 48, 16))
BF = jnp.bfloat16
F32 = jnp.float32


def dot(a, b):
    return jnp.dot(a, b, preferred_element_type=F32)


def tile_rows(bi, bj):
    start = (bi * (bi - 1) // 2 + bj) * T
    return slice(start, start + T)


def fold_rows(i):
    start = (NT * (NT - 1) // 2 + i) * T
    return slice(start, start + T)


LAST = fold_rows(NT // 2)


PIECES = (((0, 160, 80), (160, 144, 64)), ((0, 160, 80), (160, 144, 64)))
PLAN = (
    "G0", "bar", "P0", "W", "V", "grad", "G1", "P1", "G2", "S0", "ab", "G3", "S1", "W", "ab", "cd", "V",
    "ab", "cd", "W", "ab", "cd", "V", "ab", "cd", "W", "ab", "cd", "V", "ab", "cd", "W", "V", "ab", "cd",
    "gw", "W", "V", "ab", "cd", "x", "y0", "y1", "AA", "cd", "AAAAA", "cd", "BBB", "N", "BBBB", "N", "N",
)


def nt_dot(a, b):
    return lax.dot_general(a, b, (((1,), (1,)), ((), ())), preferred_element_type=F32)


def kernel(
    owner, damping, hid, grad, old, out, inv,
    h, pf, ps, pr, rs_s, rs_r, col, ys, yr, spk, w, wf, sf, x0, q1, q2, gt, av, w1, wb, yt,
    g0, inv_s, inv_r, inv_o, loc, send, recv,
):
    me = lax.axis_index("dp")
    tens = lax.axis_index("tensor")
    z, yh, c = me // 4, me // 2 % 2, me % 2

    def ring(shift):
        return lax.rem(z + shift % Z, Z)

    up = (ring(1) * 4 + yh * 2 + c, tens)
    down = (ring(-1) * 4 + yh * 2 + c, tens)
    across = (z * 4 + (1 - yh) * 2 + c, tens)
    sib = (z * 4 + yh * 2 + 1 - c, tens)
    dirs = (down, up)

    barrier = pltpu.get_barrier_semaphore()
    for device in (up, down, across, sib):
        pl.semaphore_signal(barrier, inc=1, device_id=device, device_id_type=MESH)

    sent = []

    class Message:
        def __init__(self, src, dst, device, land=None):
            n = len(sent)
            self.copy = pltpu.make_async_remote_copy(
                src_ref=src, dst_ref=dst, send_sem=send.at[n], recv_sem=recv.at[n], device_id=device, device_id_type=MESH
            )
            land = dst if land is None else land
            self.arrival = pltpu.make_async_remote_copy(
                src_ref=land, dst_ref=land, send_sem=send.at[n], recv_sem=recv.at[n], device_id=device, device_id_type=MESH
            )
            self.arrived = False
            self.copy.start()
            sent.append(self)

        def wait(self):
            self.arrived = True
            self.arrival.wait_recv()

    class Load:
        def __init__(self, src, dst, n):
            self.copy = pltpu.make_async_copy(src, dst, loc.at[n])
            self.copy.start()
            self.waited = False
            loads.append(self)

        def wait(self):
            self.waited = True
            self.copy.wait()

    loads = []
    hid_copies = []
    for q in range(4):
        block = 2 * (1 - c) + q if q < 2 else 2 * c + q - 2
        hid_copies.append(Load(hid.at[:, pl.ds(pl.multiple_of(block * B, B), B)], h.at[q], q))
    old_copy = Load(old.at[0], wf, 4)

    def columns(core, j):
        return pl.ds(pl.multiple_of((2 * core + j) * B, B), B)

    grad_copies = [Load(grad.at[:, columns(c, j)], gt.at[j, 0:COLS], 5 + j) for j in range(2)]

    row = lax.broadcasted_iota(jnp.int32, (T, T), 0)
    column = lax.broadcasted_iota(jnp.int32, (T, T), 1)

    def gram(q):
        hid_copies[q].wait()

        def put(rows, tile):
            if q < 2:
                ps[q, rows, :] = tile.astype(BF)
            else:
                pf[q - 2, rows, :] = tile

        last = jnp.zeros((T, T), F32)
        for i in range(B // 256):
            left = h[q, :, 256 * i : 256 * i + 256].T
            block = dot(left, h[q, :, 0 : 256 * i + 256])
            for a in range(2):
                bi = 2 * i + a
                for bj in range(bi):
                    put(tile_rows(bi, bj), block[T * a : T * a + T, T * bj : T * bj + T])
            lower = block[0:T, 256 * i : 256 * i + T]
            upper = block[T:, 256 * i + T :]
            put(fold_rows(i), jnp.where(row >= column, lower, upper))
            last = jnp.where(row == i, jnp.sum(jnp.where(row == column, upper, 0.0), axis=0, keepdims=True), last)
        put(LAST, last)

    def warm(lo, size, cut):
        every = slice(lo, lo + size)

        def cross(origin):
            return Message(w.at[origin, yh, c, every], w.at[origin, yh, c, every], across, land=w.at[origin, 1 - yh, c, every])

        def step(t):
            messages = []
            for d, sign in ((0, -1), (1, 1)):
                origin, arriving = ring(-sign * (t - 1)), ring(-sign * t)
                rows = every if t < 4 else (slice(lo, lo + cut), slice(lo + cut, lo + size))[d]
                messages.append(
                    Message(w.at[origin, yh, c, rows], w.at[origin, yh, c, rows], dirs[d], land=w.at[arriving, yh, c, rows])
                )
            return messages

        ringed = step(1)
        crossed = [cross(z)]
        yield
        for t in (2, 3, 4):
            for m in ringed:
                m.wait()
            ringed = step(t)
            crossed += [cross(ring(1 - t)), cross(ring(t - 1))]
            yield
        for m in ringed:
            m.wait()
        crossed.append(cross(ring(4)))
        swapped = [Message(w.at[:, yh, c, every], w.at[:, yh, c, every], sib, land=w.at[:, yh, 1 - c, every])]
        yield
        for m in crossed:
            m.wait()
        swapped.append(
            Message(w.at[:, 1 - yh, c, every], w.at[:, 1 - yh, c, every], sib, land=w.at[:, 1 - yh, 1 - c, every])
        )
        yield
        for m in swapped:
            m.wait()
        yield

    def stream(j, lo, size, cut):
        def rows_of(dest, first=0, count=size):
            return pl.ds(pl.multiple_of(dest * SHARD + lo + first, 16), count)

        def own(dest):
            rows = rows_of(dest)
            return pf[j, rows, :] + pr[j, rows, :].astype(F32)

        here = slice(lo, lo + size)
        halves = (slice(0, cut), slice(cut, size))
        placed = (slice(lo, lo + cut), slice(lo + cut, lo + size))
        part = own(ring(4)).astype(BF)
        before = []
        for d in range(2):
            rs_s[j, d, 0, placed[d], :] = part[halves[d]]
            before.append(Message(rs_s.at[j, d, 0, placed[d]], rs_r.at[j, d, 0, placed[d]], dirs[d]))
        yield
        for t in (2, 3, 4):
            after = []
            for d, sign in ((0, -1), (1, 1)):
                part = own(ring(sign * (5 - t)))
                before[d].wait()
                if t == 2:
                    rs_s[j, d, 1, placed[1 - d], :] = part[halves[1 - d]].astype(BF)
                    rs_s[j, d, 1, placed[d], :] = (part[halves[d]] + rs_r[j, d, 0, placed[d], :].astype(F32)).astype(BF)
                else:
                    rs_s[j, d, t - 1, here, :] = (part + rs_r[j, d, t - 2, here, :].astype(F32)).astype(BF)
                after.append(Message(rs_s.at[j, d, t - 1, here], rs_r.at[j, d, t - 1, here], dirs[d]))
            before = after
            yield
        part = own(z)
        for d in range(2):
            before[d].wait()
            part = part + rs_r[j, d, 3, here, :].astype(F32)
        col[j, here, :] = part
        ys[j, here, :] = part.astype(BF)
        crossed = Message(ys.at[j, here], yr.at[j, here], across)
        yield
        crossed.wait()
        spk[j, rows_of(z), :] = (col[j, here, :] + yr[j, here, :].astype(F32)).astype(BF)
        for t in (1, 2, 3, 4):
            after = []
            for d, sign in ((0, -1), (1, 1)):
                if t > 1:
                    before[d].wait()
                origin, arriving = ring(-sign * (t - 1)), ring(-sign * t)
                first, count = (0, size) if t < 4 else ((0, cut), (cut, size - cut))[d]
                src, land = rows_of(origin, first, count), rows_of(arriving, first, count)
                after.append(Message(spk.at[j, src], spk.at[j, src], dirs[d], land=spk.at[j, land]))
            before = after
            yield
        for m in before:
            m.wait()
        yield

    damp = damping[0, 0]
    tail = {}
    first_row = (z % 2) * 4 * WROWS + yh * 2 * WROWS

    def prepare():
        for name in "WV":
            for _ in runs.get(name, ()):
                pass
        for j in range(2):
            slot = owner[0, 2 * c + j]
            x0[j] = w[pl.ds(2 * slot, 2)].reshape(B, B)

    def refine(j):
        for name in piece_names[j]:
            for _ in runs.get(name, ()):
                pass
        for bi in range(NT):
            for bj in range(bi):
                tile = spk[j, tile_rows(bi, bj), :]
                sf[T * bi : T * bi + T, T * bj : T * bj + T] = tile
                sf[T * bj : T * bj + T, T * bi : T * bi + T] = tile.T
        last = spk[j, LAST, :].astype(F32)
        for i in range(NT // 2):
            tile = spk[j, fold_rows(i), :].astype(F32)
            turned = tile.T
            at = slice(256 * i, 256 * i + T)
            sf[at, at] = jnp.where(row >= column, tile, turned).astype(BF)
            at = slice(256 * i + T, 256 * i + 256)
            rest = jnp.where(row > column, turned, last[i : i + 1, :])
            sf[at, at] = jnp.where(row < column, tile, rest).astype(BF)
        yield
        left = dot(x0[j], sf[...]) * (-1.0 / TOKENS) - damp * x0[j].astype(F32)
        q1[j] = left.astype(BF)
        for i in range(NT):
            at = slice(T * i, T * i + T)
            q1[j, at, at] = (left[at, at] + jnp.where(row == column, 1.0, 0.0)).astype(BF)
        yield
        q2[j] = dot(q1[j], q1[j]).astype(BF)
        yield
        first = g0[j] + nt_dot(g0[j].astype(BF), q1[j])
        w1[...] = first
        wb[...] = first.astype(BF)
        yield
        second = w1[...] + nt_dot(wb[...], q2[j])
        w1[...] = second
        av[...] = second.astype(BF)
        yield
        wb[...] = nt_dot(av[...], q2[j]).astype(BF)
        yield
        yt[j] = (w1[...] + nt_dot(wb[...], q2[j])).astype(BF)
        store = pltpu.make_async_copy(yt.at[j, 0:COLS], out.at[:, columns(c, j)], loc.at[7 + j])
        store.start()
        tail[j] = store, Message(
            yt.at[j, COLS : 2 * COLS], out.at[:, columns(c, j)], sib, land=out.at[:, columns(1 - c, j)]
        )
        yield

    def inverse_rows():
        slot = z // 2
        block = jnp.int32(0)
        for k in range(4):
            block = jnp.where(owner[0, k] == slot, k, block)
        jj = block % 2
        shape = (2 * WROWS, B)
        unit = lax.broadcasted_iota(jnp.int32, shape, 0) + first_row == lax.broadcasted_iota(jnp.int32, shape, 1)
        mine = q1[jj, pl.ds(pl.multiple_of(first_row, 2 * WROWS), 2 * WROWS), :]
        u = jnp.where(unit, 1.0, 0.0) + mine.astype(F32)
        u = u + dot(u.astype(BF), q2[jj])
        v = dot(u.astype(BF), q2[jj])
        u = u + dot(v.astype(BF), q2[jj])
        inv_s[...] = dot(u.astype(BF), x0[jj])
        message = Message(inv_s.at[pl.ds(pl.multiple_of((1 - c) * WROWS, WROWS), WROWS)], inv_r, sib)
        yield
        message.wait()
        own_part = inv_s[pl.ds(pl.multiple_of(c * WROWS, WROWS), WROWS), :]
        inv_o[...] = jnp.where(block // 2 == c, own_part, inv_r[...])
        store = pltpu.make_async_copy(inv_o, inv.at[0], loc.at[9])
        store.start()
        yield
        store.wait()
        yield

    runs = {"N": inverse_rows(), "A": refine(0), "B": refine(1)}
    piece_names = ("ab", "cd")
    for name, piece in zip("WV", WARM):
        runs[name] = warm(*piece)
    for j in range(2):
        for name, piece in zip(piece_names[j], PIECES[j]):
            runs[name] = stream(j, *piece)
    stat = []
    released = 0
    for step in PLAN:
        if step[0] == "G":
            gram(int(step[1]))
        elif step[0] == "P":
            q = int(step[1])
            stat.append(Message(ps.at[q], pr.at[q], sib))
        elif step == "bar":
            pl.semaphore_wait(barrier, 4)
            old_copy.wait()
            w[z, yh, c] = wf[...].astype(BF)
        elif step == "x":
            prepare()
        elif step[0] == "y":
            j = int(step[1])
            g0[j] = nt_dot(gt[j], x0[j])
        elif step[0] == "S":
            stat[int(step[1])].wait()
        elif step == "grad":
            grads = [
                Message(grad.at[:, columns(1 - c, j)], gt.at[j, COLS : 2 * COLS], sib) for j in range(2)
            ]
        elif step == "gw":
            for j in range(2):
                grad_copies[j].wait()
                grads[j].wait()
        else:
            for name in step:
                next(runs.get(name, iter(())), None)
        while len(sent) - released > KEEP:
            sent[released].copy.wait_send()
            released += 1
    for j in tail:
        tail[j][0].wait()
    for load in loads:
        if not load.waited:
            load.wait()
    for message in sent:
        if not message.arrived:
            message.wait()
    for message in sent[released:]:
        message.copy.wait_send()


def body(hidden, down_grad, old_inverse, owner, damping):
    V = pltpu.VMEM
    any_space = pl.BlockSpec(memory_space=pl.ANY)
    smem = pl.BlockSpec(memory_space=pltpu.SMEM)
    result, inverse = pl.pallas_call(
        kernel,
        out_shape=(
            jax.ShapeDtypeStruct(down_grad.shape[::-1], BF),
            jax.ShapeDtypeStruct(old_inverse.shape, F32),
        ),
        in_specs=[smem, smem, any_space, any_space, any_space],
        out_specs=(any_space, any_space),
        scratch_shapes=[
            V((4, hidden.shape[0], B), BF),
            V((2, PACK, T), F32),
            V((2, PACK, T), BF),
            V((2, PACK, T), BF),
            V((2, 2, 4, SHARD, T), BF),
            V((2, 2, 4, SHARD, T), BF),
            V((2, SHARD, T), F32),
            V((2, SHARD, T), BF),
            V((2, SHARD, T), BF),
            V((2, PACK, T), BF),
            V((Z, 2, 2, WROWS, B), BF),
            V((WROWS, B), F32),
            V((B, B), BF),
            V((2, B, B), BF),
            V((2, B, B), BF),
            V((2, B, B), BF),
            V((2, 2 * COLS, B), BF),
            V((2 * COLS, B), BF),
            V((2 * COLS, B), F32),
            V((2 * COLS, B), BF),
            V((2, 2 * COLS, B), BF),
            V((2, 2 * COLS, B), F32),
            V((2 * WROWS, B), F32),
            V((WROWS, B), F32),
            V((WROWS, B), F32),
            pltpu.SemaphoreType.DMA((16,)),
            pltpu.SemaphoreType.DMA((N_MSG,)),
            pltpu.SemaphoreType.DMA((N_MSG,)),
        ],
        compiler_params=pltpu.CompilerParams(collective_id=0, has_side_effects=True, vmem_limit_bytes=60 << 20),
    )(owner, damping.reshape(1, 1), hidden, down_grad.T, old_inverse)
    return result.T, inverse


def solution(mesh):
    in_specs = (
        P("dp", "tensor"),
        P("tensor", "dp"),
        P("tensor", "dp", None),
        P("tensor", None),
        P(),
    )
    out_specs = (P("tensor", "dp"), P("tensor", "dp", None))
    return jax.shard_map(body, mesh=mesh, in_specs=in_specs, out_specs=out_specs, check_vma=False)
```
